256 devices in a mesh: img: 16 (over y, x_hi, core), ori: 16 (over z, x_lo).
Axes of the slice: x: 4 (x_hi: 2, x_lo: 2; x = x_hi * 2 + x_lo), y: 4, z: 8, core: 2. Of those that a mesh axis runs over, the one named last changes fastest.
Arguments:
- images: bfloat16 [8192, 4096], P('img'), may hold values from -6 to 6
- ctf_class: int32 [8192], P('img'), may hold values from 0 to 15
- class_mask: int32 [8192, 8], P('img'), may hold values from 0 to 1, as said below
- precision: float32 [8192], P('img'), may hold values from 0.02 to 0.5
- class_log_prior: float32 [8192, 8], P('img'), may hold values from -6 to 406
- ctf_filters: float32 [16, 4096], replicated, may hold values from -1 to 1
- volume_coef: bfloat16 [8, 16, 2, 4096], P(None, 'img'), may hold values from -6 to 6
- slice_ops: bfloat16 [8, 4096, 64], replicated, may hold values from -0.09375 to 0.09375
- tilt_index: int32 [256], P('ori'), may hold values from 0 to 7
- azimuth_index: int32 [256], P('ori'), may hold values from 0 to 31
Outputs:
- coef_sum: float32 [8, 16, 2, 4096], P(None, 'img')
- log_evidence: float32 [8192], P('img')
- class_posterior: float32 [8192, 8], P('img')
The draws below stay inside these ranges and needn't reach their ends.
Inputs may be any that keep to these rules, and one draw needn't show every extreme that they name: `class_mask`: every image allows at least one class.
All inputs are finite; a program needn't handle non-finite values.
Results may differ from the reference program's by a relative error of at most 0.024.
The reference program's roundings to bfloat16 on the way count: a program that leaves them out, or rounds other values in their place, can miss the bound.
Values may be sent and summed in bfloat16 or wider, within the bound.
A program may use at most 192 MiB of HBM per device.

```python
import math
import jax
import jax.numpy as jnp
from jax import lax

K = 8
R = 16
ORD = 64
ANG = 128
NTILT = 8
NAZI = 32
NCTF = 16
ORI_DEV = 16
LM = 4096
P_SIZE = 4096
IMAGES = 8192
ORIENT = 256
N_ORI = 16


def draw_class_mask(key, part):
    random_bits = jax.random.randint(jax.random.fold_in(key, 11), (IMAGES, K), 0, 2)
    picked = jax.random.randint(jax.random.fold_in(key, 12), (IMAGES,), 0, K)
    chosen = (picked[:, None] == jnp.arange(K)[None, :]).astype(jnp.int32)
    return jnp.maximum(random_bits, chosen).astype(jnp.int32)


def draw_class_log_prior(key, part):
    rough = jax.random.uniform(jax.random.fold_in(key, 21), (IMAGES, K), jnp.float32, -2.0, 2.0)
    lifted = jax.random.randint(jax.random.fold_in(key, 22), (IMAGES,), 0, 5) == 0
    shift = jax.random.uniform(jax.random.fold_in(key, 23), (IMAGES,), jnp.float32, 100.0, 400.0)
    rival = jax.random.randint(jax.random.fold_in(key, 24), (IMAGES,), 0, K)
    drop = jax.random.uniform(jax.random.fold_in(key, 25), (IMAGES,), jnp.float32, 1.0, 3.0)
    best = jnp.max(rough, axis=1)
    is_rival = rival[:, None] == jnp.arange(K)[None, :]
    paired = jnp.where(is_rival & lifted[:, None], (best - drop)[:, None], rough)
    lifted_rows = paired + jnp.where(lifted, shift, 0.0)[:, None]
    return lifted_rows.astype(jnp.float32)


def touch_ends(entries, own_key, least, top_value):
    longest = entries.shape.index(max(entries.shape))
    spots = []
    for shift in (0, 1):
        where = [jax.random.randint(jax.random.fold_in(own_key, axis), (), 0, length) for axis, length in enumerate(entries.shape)]
        where[longest] = (where[longest] + shift) % entries.shape[longest]
        spots.append(tuple(where))
    return entries.at[spots[0]].set(least).at[spots[1]].set(top_value)


def block_scale(stream_key, shape, shards, least, high):
    def one(dim, shards_of):
        steps = jax.random.uniform(jax.random.fold_in(jax.random.fold_in(stream_key, 6), dim), (shards_of,), jnp.float32, least / len(shards), high / len(shards))
        return jnp.repeat(jnp.exp(steps), shape[dim] // shards_of).reshape((-1,) + (1,) * (len(shape) - dim - 1))

    loudness = one(*shards[0])
    for cut in shards[1:]:
        loudness = loudness * one(*cut)
    return loudness


def gaussian(key, shape, width, limit, split=(), held_as=jnp.bfloat16):
    loudness = block_scale(key, shape, split, -0.22, 0.18) if split else 1.0
    drawn = jax.random.normal(key, shape, jnp.float32) * width * loudness
    return jnp.minimum(jnp.maximum(drawn, -limit), limit).astype(held_as)


def setup_inputs(seed: int = 0) -> dict:
    key_of = jax.random.split(jax.random.key(seed), 11)
    images = gaussian(key_of[0], (IMAGES, P_SIZE), 1.0, 6.0, ((0, 16),))
    ctf_class = touch_ends(jax.random.randint(key_of[1], (IMAGES,), 0, NCTF), jax.random.fold_in(key_of[1], 1), 0, NCTF - 1).astype(jnp.int32)
    class_mask = draw_class_mask(jax.random.fold_in(key_of[10], 71), 0)
    precision = jnp.clip(jnp.exp(math.log(0.5) - 3.218876 * jax.random.uniform(key_of[3], (IMAGES,), jnp.float32) ** block_scale(key_of[3], (IMAGES,), ((0, 16),), -0.2, 0.2)), 0.02, 0.5)
    class_log_prior = draw_class_log_prior(jax.random.fold_in(key_of[10], 71), 0)
    ctf_filters = jnp.clip(jax.random.uniform(key_of[5], (NCTF, P_SIZE), jnp.float32, -1.0, 1.0), -1.0, 1.0)
    volume_coef = gaussian(key_of[6], (K, R, 2, LM), 1.0, 6.0, ((1, 16),))
    slice_ops = gaussian(key_of[7], (NTILT, LM, ORD), LM ** -0.5, 0.09375)
    tilt_index = touch_ends(jax.random.randint(key_of[8], (ORIENT,), 0, NTILT), jax.random.fold_in(key_of[8], 1), 0, NTILT - 1).astype(jnp.int32)
    azimuth_index = touch_ends(jax.random.randint(key_of[9], (ORIENT,), 0, NAZI), jax.random.fold_in(key_of[9], 1), 0, NAZI - 1).astype(jnp.int32)
    return dict(images=images, ctf_class=ctf_class, class_mask=class_mask, precision=precision, class_log_prior=class_log_prior, ctf_filters=ctf_filters, volume_coef=volume_coef, slice_ops=slice_ops, tilt_index=tilt_index, azimuth_index=azimuth_index)


def synth_table():
    orders = (jnp.arange(ORD) - ORD // 2).astype(jnp.float32)
    angles = jnp.arange(ANG).astype(jnp.float32) * (2.0 * math.pi / ANG)
    phase = orders[:, None] * angles[None, :]
    cosine = jnp.cos(phase)
    sine = jnp.sin(phase)
    upper = jnp.concatenate([cosine, sine], axis=1)
    lower = jnp.concatenate([-sine, cosine], axis=1)
    return (jnp.concatenate([upper, lower], axis=0) * (ORD ** -0.5)).astype(jnp.bfloat16)


def rotated_ops(tilts, azimuths, slice_ops):
    chosen = jnp.take(slice_ops, tilts, axis=0).astype(jnp.float32)
    chosen = jnp.transpose(chosen, (1, 0, 2))
    orders = (jnp.arange(LM) % ORD - ORD // 2).astype(jnp.float32)
    turns = azimuths.astype(jnp.float32) * (2.0 * math.pi / NAZI)
    phase = orders[:, None] * turns[None, :]
    cosine = jnp.cos(phase)[:, :, None]
    sine = jnp.sin(phase)[:, :, None]
    upper = jnp.concatenate([cosine * chosen, -sine * chosen], axis=2)
    lower = jnp.concatenate([sine * chosen, cosine * chosen], axis=2)
    rotator = jnp.concatenate([upper, lower], axis=0)
    return rotator.reshape(2 * LM, -1).astype(jnp.bfloat16)


def synthesize(coefs, rotator, angle_table):
    classes, radial = coefs.shape[0], coefs.shape[1]
    flat_coef = coefs.reshape(classes * radial, 2 * LM)
    harmonics = jnp.dot(flat_coef, rotator, preferred_element_type=jnp.float32).astype(jnp.bfloat16)
    orients = rotator.shape[1] // (2 * ORD)
    harmonics = harmonics.reshape(classes, radial, orients, 2 * ORD).transpose(2, 0, 1, 3).reshape(-1, 2 * ORD)
    values = jnp.dot(harmonics, angle_table, preferred_element_type=jnp.float32).astype(jnp.bfloat16)
    return values.reshape(orients * classes, radial * 2 * ANG)


def adjoint(back_proj, rotator, angle_table, radial, classes):
    columns = back_proj.shape[1]
    orients = rotator.shape[1] // (2 * ORD)
    spread = back_proj.reshape(radial, 2 * ANG, columns).transpose(0, 2, 1).reshape(radial * columns, 2 * ANG)
    harmonics = jnp.dot(spread, angle_table.T, preferred_element_type=jnp.float32).astype(jnp.bfloat16)
    harmonics = harmonics.reshape(radial, orients, classes, 2 * ORD).transpose(2, 0, 1, 3)
    harmonics = harmonics.reshape(classes * radial, orients * 2 * ORD)
    return lax.dot_general(harmonics, rotator, (((1,), (1,)), ((), ())), preferred_element_type=jnp.float32)


def reference(images, ctf_class, class_mask, precision, class_log_prior, ctf_filters, volume_coef, slice_ops, tilt_index, azimuth_index):
    angle_table = synth_table()
    ctf_rows = jnp.take(ctf_filters, ctf_class, axis=0)
    filtered = (images.astype(jnp.float32) * ctf_rows).astype(jnp.bfloat16)
    ctf_square = ctf_filters * ctf_filters
    tilt_blocks = tilt_index.reshape(N_ORI, ORI_DEV)
    azimuth_blocks = azimuth_index.reshape(N_ORI, ORI_DEV)

    def forward(block):
        rotator = rotated_ops(block[0], block[1], slice_ops)
        templates = synthesize(volume_coef, rotator, angle_table)
        correl = lax.dot_general(filtered, templates, (((1,), (1,)), ((), ())), preferred_element_type=jnp.float32)
        square = templates.astype(jnp.float32)
        square = square * square
        energy = lax.dot_general(ctf_square, square, (((1,), (1,)), ((), ())), precision=lax.Precision.HIGHEST)
        return correl, energy

    correl, energy = lax.map(forward, (tilt_blocks, azimuth_blocks))
    correl = correl.transpose(1, 0, 2).reshape(IMAGES, ORIENT * K)
    energy = energy.transpose(1, 0, 2).reshape(NCTF, ORIENT * K)
    energy_rows = jnp.take(energy, ctf_class, axis=0)
    score = precision[:, None] * (correl - 0.5 * energy_rows) + jnp.tile(class_log_prior, (1, ORIENT))
    allowed = jnp.tile(class_mask, (1, ORIENT)) > 0
    score = jnp.where(allowed, score, -1e30)
    row_peak = jnp.max(score, axis=1)
    exponent = jnp.exp(score - row_peak[:, None])
    totals = exponent.reshape(IMAGES, ORIENT, K).sum(axis=1)
    norm_sum = totals.sum(axis=1)
    log_evidence = row_peak + jnp.log(norm_sum)
    class_posterior = totals / norm_sum[:, None]
    weights = (exponent / norm_sum[:, None]).astype(jnp.bfloat16)
    back_proj = lax.dot_general(filtered, weights, (((0,), (0,)), ((), ())), preferred_element_type=jnp.float32)
    back_proj = back_proj.astype(jnp.bfloat16)
    back_blocks = back_proj.reshape(P_SIZE, N_ORI, ORI_DEV * K).transpose(1, 0, 2)

    def gather_coef(running, block):
        rotator = rotated_ops(block[0], block[1], slice_ops)
        return running + adjoint(block[2], rotator, angle_table, R, K), None

    initial = jnp.zeros((K * R, 2 * LM), jnp.float32)
    coef_sum, unused = lax.scan(gather_coef, initial, (tilt_blocks, azimuth_blocks, back_blocks))
    return coef_sum.reshape(K, R, 2, LM), log_evidence, class_posterior
```

```python
import functools
import math

import jax
import jax.numpy as jnp
import numpy as np
from jax import lax
from jax.experimental import pallas as pl
from jax.experimental.pallas import tpu as pltpu
from jax.sharding import PartitionSpec as P

ORD = 64
ANG = 128
NAZI = 32
F32 = jnp.float32
BF16 = jnp.bfloat16
MESH = pl.DeviceIdType.MESH
NT = (((1,), (1,)), ((), ()))
NN = (((1,), (0,)), ((), ()))


def angle_table():
    orders = np.arange(ORD) - ORD // 2
    phase = orders[:, None] * np.arange(ANG)[None, :] * (2.0 * math.pi / ANG)
    upper = np.concatenate([np.cos(phase), np.sin(phase)], axis=1)
    lower = np.concatenate([-np.sin(phase), np.cos(phase)], axis=1)
    table = np.concatenate([upper, lower], axis=0) * ORD**-0.5
    return jnp.asarray(table.astype(np.float32)).astype(BF16)


def azimuth_table():
    orders = np.arange(2 * ORD) % ORD - ORD // 2
    phase = np.arange(NAZI)[:, None] * orders[None, :] * (2.0 * math.pi / NAZI)
    table = np.concatenate([np.cos(phase), np.sin(phase)], axis=1)
    return jnp.asarray(table.astype(np.float32))


def dot(a, b, dims, precision=None):
    return lax.dot_general(a, b, dims, precision=precision, preferred_element_type=F32)


def kernel(
    n_img,
    n_ori,
    images,
    cls_ref,
    mask_ref,
    prec_ref,
    prior_ref,
    ctf_ref,
    vol_ref,
    slices,
    tilt_ref,
    azi_ref,
    turn_ref,
    ang_ref,
    coef_ref,
    logev_ref,
    post_ref,
    img_v,
    s_v,
    x_v,
    fa_v,
    turns,
    chl,
    hbuf,
    lbuf,
    pbuf,
    hs,
    hr,
    cs,
    cr,
    cfin,
    local_sem,
    send_sem,
    recv_sem,
):
    me_a = lax.axis_index("img")
    me_o = lax.axis_index("ori")
    classes = vol_ref.shape[0]
    lm = vol_ref.shape[2]
    orients = tilt_ref.shape[0]
    rows = orients * classes
    n_images = cls_ref.shape[1]
    nctf = ctf_ref.shape[0]
    span = s_v.shape[0]
    chunk = lm // n_ori

    def partner(me, step, n):
        return lax.rem(me + step, n)

    def put(phase, src, dst, axis, other, send_slot, recv_slot):
        return pltpu.make_async_remote_copy(
            src_ref=src,
            dst_ref=dst,
            send_sem=send_sem.at[phase, send_slot],
            recv_sem=recv_sem.at[phase, recv_slot],
            device_id={axis: other},
            device_id_type=MESH,
        )

    fetch_s = pltpu.make_async_copy(slices, s_v, local_sem.at[0])
    fetch_s.start()
    fetch_i = pltpu.make_async_copy(images, img_v, local_sem.at[1])
    fetch_i.start()

    barrier = pltpu.get_barrier_semaphore()

    def greet(axis, me, n):
        def one(step, carry):
            pl.semaphore_signal(
                barrier, inc=1, device_id={axis: partner(me, step, n)}, device_id_type=MESH
            )
            return carry

        lax.fori_loop(1, n, one, 0)

    greet("img", me_a, n_img)
    greet("ori", me_o, n_ori)

    v_re = vol_ref[:, 0, :].astype(F32)
    v_im = vol_ref[:, 1, :].astype(F32)

    def rotate(o, carry):
        turn = turn_ref[pl.ds(azi_ref[o], 1), :]
        cos8 = jnp.broadcast_to(turn[:, :ANG], (classes, ANG))
        sin8 = jnp.broadcast_to(turn[:, ANG:], (classes, ANG))
        turns[o, 0] = cos8
        turns[o, 1] = sin8
        for j in range(lm // ANG):
            cols = slice(j * ANG, (j + 1) * ANG)
            re, im = v_re[:, cols], v_im[:, cols]
            both = jnp.concatenate([re * cos8 + im * sin8, im * cos8 - re * sin8], axis=0)
            x_v[pl.ds(pl.multiple_of(o * 16, 16), 16), cols] = both.astype(BF16)
        return carry

    lax.fori_loop(0, orients, rotate, 0)

    fetch_s.wait()
    spread = dot(x_v[...], s_v[...], NT).reshape(orients, 2, classes, span)
    lane = lax.broadcasted_iota(jnp.int32, (classes, span), 1) // ORD
    low = lax.broadcasted_iota(jnp.int32, (classes, 2 * ORD), 1) < ORD
    parts = []
    for o in range(orients):
        chosen = lane == tilt_ref[o]
        halves = []
        for c in range(2):
            kept = jnp.where(chosen, spread[o, c], 0.0)
            fold = kept[:, : 2 * ORD]
            for b in range(1, span // (2 * ORD)):
                fold = fold + kept[:, b * 2 * ORD : (b + 1) * 2 * ORD]
            halves.append(fold + pltpu.roll(fold, ORD, 1))
        parts.append(jnp.where(low, halves[0], halves[1]))
    harm = jnp.concatenate(parts, axis=0).astype(BF16)
    ang = ang_ref[...]
    temp = dot(harm, ang, NN).astype(BF16).astype(F32)
    own = pl.ds(pl.multiple_of(me_a * 2 * ANG, 2 * ANG), 2 * ANG)
    ctf_own = ctf_ref[:, own]
    energy_own = dot(ctf_own * ctf_own, temp * temp, NT, lax.Precision.HIGHEST)
    e_hi = energy_own.astype(BF16)
    e_lo = (energy_own - e_hi.astype(F32)).astype(BF16)
    hbuf[me_a, 0:rows, :] = harm
    hbuf[me_a, rows : rows + nctf, :] = e_hi
    hbuf[me_a, rows + nctf : rows + 2 * nctf, :] = e_lo

    pl.semaphore_wait(barrier, n_img - 1 + n_ori - 1)

    def send_harm(step, carry):
        to = partner(me_a, step, n_img)
        put(0, hbuf.at[me_a], hbuf.at[me_a], "img", to, step, me_a).start()
        return carry

    lax.fori_loop(1, n_img, send_harm, 0)

    ctf_hi = ctf_ref[...].astype(BF16)
    chl[0:nctf, :] = ctf_hi
    chl[nctf : 2 * nctf, :] = (ctf_ref[...] - ctf_hi.astype(F32)).astype(BF16)
    cls = cls_ref[...]
    hot2 = lax.rem(lax.broadcasted_iota(jnp.int32, (2 * nctf, n_images), 0), nctf) == cls
    hot2 = jnp.where(hot2, 1.0, 0.0).T.astype(BF16)
    fetch_i.wait()

    def shell(r, carry):
        cols = pl.ds(pl.multiple_of(r * 2 * ANG, 2 * ANG), 2 * ANG)
        ctf_rows = dot(hot2, chl[:, cols], NN)
        filtered = (img_v[:, cols].astype(F32) * ctf_rows).astype(BF16)
        proj = dot(filtered, ang, NT).astype(BF16)
        fa_v[:, pl.ds(pl.multiple_of(r * 2 * ORD, 2 * ORD), 2 * ORD)] = proj
        return carry

    lax.fori_loop(0, n_img, shell, 0)

    def take_harm(step, carry):
        sender = partner(me_a, step, n_img)
        put(0, hbuf.at[sender], hbuf.at[sender], "img", sender, step, sender).wait_recv()
        return carry

    lax.fori_loop(1, n_img, take_harm, 0)
    all_harm = jnp.concatenate([hbuf[r, 0:rows, :] for r in range(n_img)], axis=1)
    correl = dot(all_harm, fa_v[...], NT)
    energy = jnp.zeros((nctf, rows), F32)
    for r in range(n_img):
        energy = energy + hbuf[r, rows : rows + nctf, :].astype(F32)
        energy = energy + hbuf[r, rows + nctf : rows + 2 * nctf, :].astype(F32)
    hot = jnp.where(lax.broadcasted_iota(jnp.int32, (nctf, n_images), 0) == cls, 1.0, 0.0)
    energy_rows = dot(energy.T, hot, NN, lax.Precision.HIGHEST)
    score = prec_ref[...] * (correl - 0.5 * energy_rows)
    score = score.reshape(orients, classes, n_images) + prior_ref[...][None]
    score = jnp.where((mask_ref[...] > 0)[None], score, -1e30)
    peak = jnp.max(jnp.max(score, axis=0), axis=0, keepdims=True)
    exponent = jnp.exp(score - peak[None])
    totals = jnp.sum(exponent, axis=0)
    local_lse = peak + jnp.log(jnp.sum(totals, axis=0, keepdims=True))
    lbuf[me_o] = local_lse

    def send_lse(step, carry):
        to = partner(me_o, step, n_ori)
        put(1, lbuf.at[me_o], lbuf.at[me_o], "ori", to, step, me_o).start()
        return carry

    lax.fori_loop(1, n_ori, send_lse, 0)

    def take_lse(step, carry):
        sender = partner(me_o, step, n_ori)
        put(1, lbuf.at[sender], lbuf.at[sender], "ori", sender, step, sender).wait_recv()
        return carry

    lax.fori_loop(1, n_ori, take_lse, 0)
    all_lse = lbuf[...]
    top = jnp.max(all_lse, axis=0)
    lse = top + jnp.log(jnp.sum(jnp.exp(all_lse - top[None]), axis=0))
    logev_ref[...] = lse
    scale = jnp.exp(peak - lse)
    weights = (exponent * scale[None]).reshape(rows, n_images).astype(BF16)

    def back(step, carry):
        to = partner(me_a, step, n_img)
        cols = pl.ds(pl.multiple_of(to * 2 * ORD, 2 * ORD), 2 * ORD)
        hs[to] = dot(weights, fa_v[:, cols], NN).astype(BF16)

        @pl.when(step < n_img)
        def _():
            put(2, hs.at[to], hr.at[me_a], "img", to, step, me_a).start()

        return carry

    lax.fori_loop(1, n_img + 1, back, 0)

    share = totals * scale
    half = n_images // 2
    share = jnp.concatenate([share[:, :half], share[:, half:]], axis=0)
    pbuf[me_o] = share.astype(BF16)

    def send_share(step, carry):
        to = partner(me_o, step, n_ori)
        put(3, pbuf.at[me_o], pbuf.at[me_o], "ori", to, step, me_o).start()
        return carry

    lax.fori_loop(1, n_ori, send_share, 0)

    def take_back(step, total):
        sender = partner(me_a, step, n_img)
        put(2, hs.at[sender], hr.at[sender], "img", sender, step, sender).wait_recv()
        return total + hr[sender].astype(F32)

    summed = lax.fori_loop(1, n_img, take_back, hs[me_a].astype(F32))
    summed = summed.astype(BF16).astype(F32)

    blocks = []
    for o in range(orients):
        piece = summed[o * classes : (o + 1) * classes, :]
        turned = pltpu.roll(piece, ORD, 1)
        chosen = lane == tilt_ref[o]
        for both in (jnp.where(low, piece, turned), jnp.where(low, turned, piece)):
            wide = jnp.concatenate([both] * (span // (2 * ORD)), axis=1)
            blocks.append(jnp.where(chosen, wide, 0.0))
    placed = jnp.concatenate(blocks, axis=0).astype(BF16)
    cos_all = jnp.concatenate([turns[:, 0]] * (chunk // ANG), axis=2)
    sin_all = jnp.concatenate([turns[:, 1]] * (chunk // ANG), axis=2)

    def coef(step, carry):
        to = partner(me_o, step, n_ori)
        cols = pl.ds(pl.multiple_of(to * chunk, chunk), chunk)
        wide = dot(placed, s_v[:, cols], NN).reshape(orients, 2, classes, chunk)
        re, im = wide[:, 0], wide[:, 1]
        out_re = jnp.sum(re * cos_all - im * sin_all, axis=0)
        out_im = jnp.sum(re * sin_all + im * cos_all, axis=0)
        cs[to] = jnp.concatenate([out_re, out_im], axis=0).astype(BF16)

        @pl.when(step < n_ori)
        def _():
            put(4, cs.at[to], cr.at[me_o], "ori", to, step, me_o).start()

        return carry

    lax.fori_loop(1, n_ori + 1, coef, 0)

    def take_coef(step, total):
        sender = partner(me_o, step, n_ori)
        put(4, cs.at[sender], cr.at[sender], "ori", sender, step, sender).wait_recv()
        return total + cr[sender].astype(F32)

    total = lax.fori_loop(1, n_ori, take_coef, cs[me_o].astype(F32))
    cfin[me_o] = total.astype(BF16)

    def send_final(step, carry):
        to = partner(me_o, step, n_ori)
        put(5, cfin.at[me_o], cfin.at[me_o], "ori", to, step, me_o).start()
        return carry

    lax.fori_loop(1, n_ori, send_final, 0)

    def take_share(step, total):
        sender = partner(me_o, step, n_ori)
        put(3, pbuf.at[sender], pbuf.at[sender], "ori", sender, step, sender).wait_recv()
        return total + pbuf[sender].astype(F32)

    share = lax.fori_loop(1, n_ori, take_share, share)
    post_ref[...] = jnp.concatenate([share[:classes], share[classes:]], axis=1)

    def take_final(step, carry):
        sender = partner(me_o, step, n_ori)
        put(5, cfin.at[sender], cfin.at[sender], "ori", sender, step, sender).wait_recv()
        return carry

    lax.fori_loop(1, n_ori, take_final, 0)
    for j in range(n_ori):
        coef_ref[:, j * chunk : (j + 1) * chunk] = cfin[j].astype(F32)

    def drain(step, carry):
        to = partner(me_a, step, n_img)
        put(0, hbuf.at[me_a], hbuf.at[me_a], "img", to, step, me_a).wait_send()
        put(2, hs.at[to], hr.at[me_a], "img", to, step, me_a).wait_send()
        return carry

    lax.fori_loop(1, n_img, drain, 0)

    def drain_ori(step, carry):
        to = partner(me_o, step, n_ori)
        put(1, lbuf.at[me_o], lbuf.at[me_o], "ori", to, step, me_o).wait_send()
        put(3, pbuf.at[me_o], pbuf.at[me_o], "ori", to, step, me_o).wait_send()
        put(4, cs.at[to], cr.at[me_o], "ori", to, step, me_o).wait_send()
        put(5, cfin.at[me_o], cfin.at[me_o], "ori", to, step, me_o).wait_send()
        return carry

    lax.fori_loop(1, n_ori, drain_ori, 0)


def body(
    n_img,
    n_ori,
    images,
    ctf_class,
    class_mask,
    precision,
    class_log_prior,
    ctf_filters,
    volume_coef,
    slice_ops,
    tilt_index,
    azimuth_index,
):
    n_images, size = images.shape
    classes, lm = volume_coef.shape[0], volume_coef.shape[3]
    tilts = slice_ops.shape[0]
    orients = tilt_index.shape[0]
    nctf = ctf_filters.shape[0]
    rows = orients * classes
    span = tilts * ORD
    chunk = lm // n_ori
    slots = max(n_img, n_ori)
    vmem = pl.BlockSpec(memory_space=pltpu.VMEM)
    smem = pl.BlockSpec(memory_space=pltpu.SMEM)
    anywhere = pl.BlockSpec(memory_space=pl.ANY)
    coef, logev, post = pl.pallas_call(
        functools.partial(kernel, n_img, n_ori),
        out_shape=(
            jax.ShapeDtypeStruct((2 * classes, lm), F32),
            jax.ShapeDtypeStruct((1, n_images), F32),
            jax.ShapeDtypeStruct((classes, n_images), F32),
        ),
        in_specs=[anywhere, vmem, vmem, vmem, vmem, vmem, vmem, anywhere, smem, smem, vmem, vmem],
        out_specs=(vmem, vmem, vmem),
        scratch_shapes=[
            pltpu.VMEM((n_images, size), BF16),
            pltpu.VMEM((span, lm), BF16),
            pltpu.VMEM((2 * rows, lm), BF16),
            pltpu.VMEM((n_images, n_img * 2 * ORD), BF16),
            pltpu.VMEM((orients, 2, classes, ANG), F32),
            pltpu.VMEM((2 * nctf, size), BF16),
            pltpu.VMEM((n_img, rows + 2 * nctf, 2 * ORD), BF16),
            pltpu.VMEM((n_ori, 1, n_images), F32),
            pltpu.VMEM((n_ori, 2 * classes, n_images // 2), BF16),
            pltpu.VMEM((n_img, rows, 2 * ORD), BF16),
            pltpu.VMEM((n_img, rows, 2 * ORD), BF16),
            pltpu.VMEM((n_ori, 2 * classes, chunk), BF16),
            pltpu.VMEM((n_ori, 2 * classes, chunk), BF16),
            pltpu.VMEM((n_ori, 2 * classes, chunk), BF16),
            pltpu.SemaphoreType.DMA((2,)),
            pltpu.SemaphoreType.DMA((6, slots)),
            pltpu.SemaphoreType.DMA((6, slots)),
        ],
        compiler_params=pltpu.CompilerParams(
            collective_id=0, has_side_effects=True, vmem_limit_bytes=50 * 2**20
        ),
        cost_estimate=pl.CostEstimate(
            flops=4 * 10**9, bytes_accessed=10**7, transcendentals=10**5
        ),
    )(
        images,
        ctf_class.reshape(1, n_images),
        class_mask.T,
        precision.reshape(1, n_images),
        class_log_prior.T,
        ctf_filters,
        volume_coef.reshape(classes, 2, lm),
        slice_ops.transpose(0, 2, 1).reshape(span, lm),
        tilt_index,
        azimuth_index,
        azimuth_table(),
        angle_table(),
    )
    coef_sum = coef.reshape(2, classes, 1, lm).transpose(1, 2, 0, 3)
    return coef_sum, logev.reshape(n_images), post.T


def solution(mesh):
    placed = (
        P("img", None),
        P("img"),
        P("img", None),
        P("img"),
        P("img", None),
        P(),
        P(None, "img", None, None),
        P(),
        P("ori"),
        P("ori"),
    )
    return jax.shard_map(
        functools.partial(body, mesh.shape["img"], mesh.shape["ori"]),
        mesh=mesh,
        in_specs=placed,
        out_specs=(P(None, "img", None, None), P("img"), P("img", None)),
        check_vma=False,
    )
```
